32 devices in a mesh: dp: 16 (over z, y, x), own: 2 (over core).
Axes of the slice: x: 2, y: 2, z: 4, core: 2. Of those that a mesh axis runs over, the one named last changes fastest.
Arguments:
- tokens: bfloat16 [16384, 1024], P(('dp', 'own')), may hold values from -6 to 6
- cotangent: bfloat16 [16384, 1024], P(('dp', 'own')), may hold values from -6 to 6
- slot_table: int32 [12], replicated, may hold values from 0 to 11, as said below
- matrix_master: float32 [12, 1024, 1024], P('own')
- matrix_momentum: float32 [12, 1024, 1024], P('own')
- vector_params: float32 [12, 1024], replicated
- vector_first: float32 [12, 1024], replicated
- vector_second: float32 [12, 1024], replicated, as said below
Outputs:
- activations: float32 [16384, 1024], P(('dp', 'own'))
- input_grad: float32 [16384, 1024], P(('dp', 'own'))
- new_master: float32 [12, 1024, 1024], P('own')
- new_momentum: float32 [12, 1024, 1024], P('own')
- new_vector_params: float32 [12, 1024], replicated
- new_vector_first: float32 [12, 1024], replicated
- new_vector_second: float32 [12, 1024], replicated
The draws below stay inside these ranges and needn't reach their ends.
Inputs may be any that keep to these rules, and one draw needn't show every extreme that they name: Block b (query, key, value, output projection, then the 4 column blocks of the up projection, then the 4 row blocks of the down projection) lives in slot slot_table[b]; the values are distinct and slot 11 is always named. `vector_second`: positive.
All inputs are finite; a program needn't handle non-finite values.
Results may differ from the reference program's by a relative error of at most 0.035.
Values may be sent and summed in bfloat16 or wider, within the bound.
A program may use at most 384 MiB of HBM per device.

```python
import math
import jax
import jax.numpy as jnp
from jax import lax

D = 1024
HEADS = 16
HEAD = 64
FF = 4096
LEN = 512
NEWTON_STEPS = 5
STEP = 10
TOKENS = 16384
BLOCKS = 12
SLOTS_ALL = 12
VEC = 12


def table_common(key):
    key = jax.random.fold_in(key, 101)
    first_key, second_key = jax.random.split(key)
    picked = jax.random.permutation(first_key, SLOTS_ALL - 1)[:BLOCKS - 1]
    chosen = jnp.concatenate([picked.astype(jnp.int32), jnp.full((1,), SLOTS_ALL - 1, jnp.int32)])
    return jax.random.permutation(second_key, chosen).astype(jnp.int32)


def row_scales():
    hidden_blocks = FF // D
    return jnp.array([0.05, 0.3, 0.7, 0.7, 0.7, 0.7, 0.7, 0.7] + [0.5] * hidden_blocks, jnp.float32) * math.sqrt(TOKENS)


def draw_slot_table(key, part):
    return table_common(key)


def draw_matrix_master(key, part):
    table = table_common(key)
    key = jax.random.fold_in(key, 2)
    hidden_blocks = FF // D
    fans = [D, D, D // 16, D // 8] + [D] * hidden_blocks + [FF] * hidden_blocks
    block_scale = jnp.array([fan ** (-0.5) for fan in fans], jnp.float32)
    match = table[None, :] == jnp.arange(SLOTS_ALL, dtype=jnp.int32)[:, None]
    slot_scale = jnp.where(jnp.any(match, axis=1), jnp.sum(jnp.where(match, block_scale[None, :], 0.0), axis=1), D ** (-0.5))
    noise = jax.random.truncated_normal(key, -6.0, 6.0, (SLOTS_ALL, D, D), jnp.float32)
    return noise * slot_scale[:, None, None]


def draw_matrix_momentum(key, part):
    key = jax.random.fold_in(key, 3)
    noise = jax.random.truncated_normal(key, -6.0, 6.0, (SLOTS_ALL, D, D), jnp.float32)
    return noise * (0.4 * math.sqrt(TOKENS))


def draw_vector_params(key, part):
    key = jax.random.fold_in(key, 5)
    first_key, second_key = jax.random.split(key)
    hidden_blocks = FF // D
    is_gain = jnp.array([0, 0, 0, 0, 1, 0, 1, 0] + [0] * hidden_blocks, jnp.float32)
    noise = jax.random.truncated_normal(first_key, -6.0, 6.0, (VEC, D), jnp.float32)
    spread = jax.random.uniform(second_key, (VEC, D), jnp.float32, -1.0, 1.0)
    return jnp.where(is_gain[:, None] > 0.5, 1.0 + 0.2 * spread, 0.1 * noise)


def draw_vector_first(key, part):
    key = jax.random.fold_in(key, 7)
    noise = jax.random.truncated_normal(key, -6.0, 6.0, (VEC, D), jnp.float32)
    return noise * (0.11 * row_scales())[:, None]


def draw_vector_second(key, part):
    key = jax.random.fold_in(key, 9)
    factor = jnp.exp(jax.random.uniform(key, (VEC, D), jnp.float32, math.log(0.5), math.log(8.0)))
    scale = row_scales()
    return factor * (0.001 * scale * scale)[:, None]


def level_of(own_key, shape, cuts, least, largest):
    loudness, own = 1.0, jax.random.fold_in(own_key, 6)
    for dim, parts in cuts:
        steps = jnp.exp(jax.random.uniform(jax.random.fold_in(own, dim), (parts,), jnp.float32, least / len(cuts), largest / len(cuts)))
        loudness = loudness * jnp.repeat(steps, shape[dim] // parts).reshape([-1 if axis == dim else 1 for axis in range(len(shape))])
    return loudness


def scatter_about(rng, extent, scale, bound, shards=(), kind=jnp.bfloat16):
    level = level_of(rng, extent, shards, -0.22, 0.18) if shards else 1.0
    result = jax.random.normal(rng, extent, jnp.float32) * scale * level
    return jnp.minimum(jnp.maximum(result, -bound), bound).astype(kind)


def setup_inputs(seed: int = 0) -> dict:
    splits = jax.random.split(jax.random.key(seed), 9)
    tokens = scatter_about(splits[0], (TOKENS, D), 1.0, 6.0, ((0, 32),))
    cotangent = scatter_about(splits[1], (TOKENS, D), 1.0, 6.0, ((0, 32),))
    slot_table = draw_slot_table(jax.random.fold_in(splits[8], 71), 0)
    matrix_master = draw_matrix_master(jax.random.fold_in(splits[8], 71), 0)
    matrix_momentum = draw_matrix_momentum(jax.random.fold_in(splits[8], 71), 0)
    vector_params = draw_vector_params(jax.random.fold_in(splits[8], 71), 0)
    vector_first = draw_vector_first(jax.random.fold_in(splits[8], 71), 0)
    vector_second = draw_vector_second(jax.random.fold_in(splits[8], 71), 0)
    return dict(tokens=tokens, cotangent=cotangent, slot_table=slot_table, matrix_master=matrix_master, matrix_momentum=matrix_momentum, vector_params=vector_params, vector_first=vector_first, vector_second=vector_second)


@jax.custom_vjp
def low(v):
    return lax.optimization_barrier(v.astype(jnp.bfloat16)).astype(jnp.float32)

@jax.custom_vjp
def low_back(v):
    return v

def low_keep(v):
    return (low(v), None)

def low_pass(kept, grad):
    return (grad,)

def back_keep(v):
    return (v, None)

def back_low(kept, grad):
    return (low(grad),)
low.defvjp(low_keep, low_pass)
low_back.defvjp(back_keep, back_low)
poly_first = 3.4445
poly_second = -4.775
poly_third = 2.0315
momentum_decay = 0.95
matrix_rate = 1.0
matrix_decay = 0.01
beta_first = 0.9
beta_second = 0.999
vector_rate = 0.2
vector_decay = 0.01
adam_epsilon = 1e-08
norm_epsilon = 1e-05
ortho_epsilon = 1e-07

def round_both(values):
    return low(low_back(values))

def rounded(values):
    return lax.optimization_barrier(values.astype(jnp.bfloat16)).astype(jnp.float32)

def matmul(operand_left, operand_right):
    return jnp.dot(operand_left, operand_right, precision=lax.Precision.HIGHEST, preferred_element_type=jnp.float32)

def layer_norm(values, gain_row, shift_row):
    centred = values - lax.optimization_barrier(jnp.mean(values, axis=-1, keepdims=True))
    spread = lax.optimization_barrier(jnp.mean(centred * centred, axis=-1, keepdims=True))
    return centred * lax.rsqrt(spread + norm_epsilon) * gain_row + shift_row

def gelu_exact(values):
    return 0.5 * values * (1.0 + jax.scipy.special.erf(values * (1.0 / math.sqrt(2.0))))

def attend(triple):
    queries, key_rows, values = triple
    length = queries.shape[0]
    query_heads = queries.reshape(length, HEADS, HEAD)
    key_heads = key_rows.reshape(length, HEADS, HEAD)
    value_heads = values.reshape(length, HEADS, HEAD)
    scores = jnp.einsum('qhd,khd->hqk', query_heads, key_heads, precision=lax.Precision.HIGHEST)
    scores = low_back(scores * (1.0 / math.sqrt(HEAD)))
    row_peak = lax.optimization_barrier(jnp.max(scores, axis=-1, keepdims=True))
    exps = jnp.exp(scores - row_peak)
    probabilities = exps / lax.optimization_barrier(jnp.sum(exps, axis=-1, keepdims=True))
    mixed = jnp.einsum('hqk,khd->qhd', low(probabilities), value_heads, precision=lax.Precision.HIGHEST)
    return mixed.reshape(length, HEADS * HEAD)

def forward(inputs, w_query, w_key, w_value, w_out, w_up, w_down, vectors):
    features = inputs.shape[1]
    hidden_blocks = vectors.shape[0] - 8
    bias_up = vectors[8:].reshape(hidden_blocks * features)
    queries = round_both(matmul(inputs, w_query) + vectors[0])
    key_rows = round_both(matmul(inputs, w_key))
    values = round_both(matmul(inputs, w_value) + vectors[1])
    sequences = inputs.shape[0] // LEN
    attended = lax.map(jax.checkpoint(attend), (queries.reshape(sequences, LEN, features), key_rows.reshape(sequences, LEN, features), values.reshape(sequences, LEN, features)))
    mixed_rows = round_both(attended.reshape(sequences * LEN, features))
    attn_out = low_back(matmul(mixed_rows, w_out) + vectors[2])
    normed = layer_norm(inputs + attn_out, vectors[4], vectors[5])
    pre_hidden = low_back(matmul(low(normed), w_up) + bias_up)
    activity = low(gelu_exact(pre_hidden))
    branch = low_back(matmul(activity, w_down) + vectors[3])
    return layer_norm(normed + branch, vectors[6], vectors[7])

def orthogonal(momentum):
    iterate = momentum / (jnp.sqrt(jnp.sum(momentum * momentum)) + ortho_epsilon)
    for sweep in range(NEWTON_STEPS):
        low_iter = rounded(iterate)
        gram = matmul(low_iter, low_iter.T)
        gram_low = rounded(gram)
        square = matmul(gram_low, gram_low)
        poly = rounded(poly_second * gram + poly_third * square)
        iterate = poly_first * iterate + matmul(poly, low_iter)
    return iterate

def reference(tokens, cotangent, slot_table, matrix_master, matrix_momentum, vector_params, vector_first, vector_second):
    features = tokens.shape[1]
    hidden_blocks = vector_params.shape[0] - 8
    slot_count = matrix_master.shape[0]
    weights = rounded(matrix_master)
    blocks = weights[slot_table]
    w_up = jnp.concatenate([blocks[4 + column] for column in range(hidden_blocks)], axis=1)
    w_down = jnp.concatenate([blocks[4 + hidden_blocks + column] for column in range(hidden_blocks)], axis=0)
    params = (blocks[0], blocks[1], blocks[2], blocks[3], w_up, w_down, vector_params)
    sequences = tokens.shape[0] // LEN
    group_size = 8 if sequences % 8 == 0 else 1
    rounds = sequences // group_size
    inputs = tokens.astype(jnp.float32).reshape(rounds, group_size * LEN, features)
    pulled = cotangent.astype(jnp.float32).reshape(rounds, group_size * LEN, features)

    def one_group(totals, pair_rows):
        outputs, pullback = jax.vjp(forward, pair_rows[0], *params)
        gradients = pullback(pair_rows[1])
        return (jax.tree.map(jnp.add, totals, tuple(gradients[1:])), (outputs, gradients[0]))
    totals, (activations, input_grad) = lax.scan(one_group, jax.tree.map(jnp.zeros_like, params), (inputs, pulled))
    grad_query, grad_key, grad_value, grad_out, grad_up, grad_down, vector_grad = totals
    grad_blocks = jnp.stack([grad_query, grad_key, grad_value, grad_out] + [grad_up[:, column * features:(column + 1) * features] for column in range(hidden_blocks)] + [grad_down[column * features:(column + 1) * features] for column in range(hidden_blocks)])
    match = slot_table[None, :] == jnp.arange(slot_count, dtype=jnp.int32)[:, None]
    slot_used = jnp.any(match, axis=1)
    slot_grad = jnp.einsum('sb,brc->src', match.astype(jnp.float32), grad_blocks, precision=lax.Precision.HIGHEST)
    new_momentum = momentum_decay * matrix_momentum + slot_grad
    ortho = jnp.where(slot_used[:, None, None], lax.map(orthogonal, new_momentum), 0.0)
    new_master = matrix_master - matrix_rate * (ortho + matrix_decay * matrix_master)
    new_first = beta_first * vector_first + (1.0 - beta_first) * vector_grad
    new_second = beta_second * vector_second + (1.0 - beta_second) * vector_grad * vector_grad
    first_hat = new_first / (1.0 - beta_first ** STEP)
    second_hat = new_second / (1.0 - beta_second ** STEP)
    new_params = vector_params - vector_rate * (first_hat / (jnp.sqrt(second_hat) + adam_epsilon) + vector_decay * vector_params)
    return (activations.reshape(-1, features), input_grad.reshape(-1, features), new_master, new_momentum, new_params, new_first, new_second)
```

```python
import math

import jax
import jax.numpy as jnp
from jax import lax
from jax.experimental import pallas as pl
from jax.experimental.pallas import tpu as pltpu
from jax.sharding import PartitionSpec as P

HEADS = 16
HEAD = 64
LEN = 512
NEWTON_STEPS = 5
STEP = 10


poly_first = 3.4445
poly_second = -4.775
poly_third = 2.0315
momentum_decay = 0.95
matrix_rate = 1.0
matrix_decay = 0.01
beta_first = 0.9
beta_second = 0.999
vector_rate = 0.2
vector_decay = 0.01
adam_epsilon = 1e-08
norm_epsilon = 1e-05
ortho_epsilon = 1e-07


def layer_norm(values, gain_row, shift_row):
    centred = values - jnp.mean(values, axis=-1, keepdims=True)
    spread = jnp.mean(centred * centred, axis=-1, keepdims=True)
    return centred * lax.rsqrt(spread + norm_epsilon) * gain_row + shift_row


def gelu_exact(values):
    return 0.5 * values * (1.0 + jax.scipy.special.erf(values * (1.0 / math.sqrt(2.0))))


def contract_last(operand_left, operand_right):
    return lax.dot_general(
        operand_left, operand_right, (((1,), (1,)), ((), ())), preferred_element_type=jnp.float32
    )


def contract_first(operand_left, operand_right):
    return lax.dot_general(
        operand_left, operand_right, (((0,), (0,)), ((), ())), preferred_element_type=jnp.float32
    )


def head_scores(queries, key_rows):
    length = queries.shape[0]
    query_heads = queries.reshape(length, HEADS, HEAD)
    key_heads = key_rows.reshape(length, HEADS, HEAD)
    scores = jnp.einsum("qhd,khd->hqk", query_heads, key_heads, preferred_element_type=jnp.float32)
    return (scores * (1.0 / math.sqrt(HEAD)), query_heads, key_heads)


def attend_forward(triple):
    queries, key_rows, values = triple
    length = queries.shape[0]
    scores, query_heads, key_heads = head_scores(queries, key_rows)
    row_peak = jnp.max(scores, axis=-1, keepdims=True)
    exps = jnp.exp(scores - row_peak)
    row_total = jnp.sum(exps, axis=-1, keepdims=True)
    probabilities = (exps / row_total).astype(jnp.bfloat16)
    value_heads = values.reshape(length, HEADS, HEAD)
    mixed = jnp.einsum(
        "hqk,khd->qhd", probabilities, value_heads, preferred_element_type=jnp.float32
    )
    return (mixed.reshape(length, HEADS * HEAD).astype(jnp.bfloat16), row_peak, row_total)


def attend_backward(bundle):
    queries, key_rows, values, grad_mixed, row_peak, row_total = bundle
    length = queries.shape[0]
    scores, query_heads, key_heads = head_scores(queries, key_rows)
    probabilities = jnp.exp(scores - row_peak) / row_total
    value_heads = values.reshape(length, HEADS, HEAD)
    grad_heads = grad_mixed.reshape(length, HEADS, HEAD)
    grad_probs = jnp.einsum(
        "qhd,khd->hqk", grad_heads, value_heads, preferred_element_type=jnp.float32
    )
    row_dot = jnp.sum(grad_probs * probabilities, axis=-1, keepdims=True)
    grad_scores = (probabilities * (grad_probs - row_dot)).astype(jnp.bfloat16)
    scale = 1.0 / math.sqrt(HEAD)
    grad_query = (
        jnp.einsum("hqk,khd->qhd", grad_scores, key_heads, preferred_element_type=jnp.float32)
        * scale
    )
    grad_key = (
        jnp.einsum("hqk,qhd->khd", grad_scores, query_heads, preferred_element_type=jnp.float32)
        * scale
    )
    grad_value = jnp.einsum(
        "hqk,qhd->khd",
        probabilities.astype(jnp.bfloat16),
        grad_heads,
        preferred_element_type=jnp.float32,
    )
    features = HEADS * HEAD
    return tuple(
        grad.reshape(length, features).astype(jnp.bfloat16)
        for grad in (grad_query, grad_key, grad_value)
    )


def newton_kernel(momentum_ref, ortho_ref, iterate, low_iter, gram, gram_low, poly):
    size = momentum_ref.shape[0]
    tile = min(512, size)
    tiles = size // tile

    def total_step(place, total):
        rows = momentum_ref[pl.ds(pl.multiple_of(place * 128, 128), 128), :]
        return total + jnp.sum(rows * rows)

    total = lax.fori_loop(0, size // 128, total_step, jnp.float32(0.0))
    norm = jnp.sqrt(jnp.full((8, 128), total, jnp.float32)) + ortho_epsilon
    inverse = (1.0 / norm)[0:1, 0:1]

    def rows_at(place):
        return pl.ds(pl.multiple_of(place * tile, tile), tile)

    @pl.loop(0, tiles)
    def _(place):
        rows = rows_at(place)
        start = momentum_ref[rows, :] * inverse
        iterate[rows, :] = start
        low_iter[rows, :] = start.astype(jnp.bfloat16)

    @pl.loop(0, NEWTON_STEPS)
    def _(sweep):
        @pl.loop(0, tiles)
        def _(place):
            rows = rows_at(place)
            product = contract_last(low_iter[rows, :], low_iter[...])
            gram[rows, :] = product
            gram_low[rows, :] = product.astype(jnp.bfloat16)

        @pl.loop(0, tiles)
        def _(place):
            rows = rows_at(place)
            square = jnp.dot(
                gram_low[rows, :], gram_low[...], preferred_element_type=jnp.float32
            )
            poly[rows, :] = (poly_second * gram[rows, :] + poly_third * square).astype(
                jnp.bfloat16
            )

        @pl.loop(0, tiles)
        def _(place):
            rows = rows_at(place)
            iterate[rows, :] = poly_first * iterate[rows, :] + jnp.dot(
                poly[rows, :], low_iter[...], preferred_element_type=jnp.float32
            )

        @pl.loop(0, tiles)
        def _(place):
            rows = rows_at(place)
            low_iter[rows, :] = iterate[rows, :].astype(jnp.bfloat16)

    ortho_ref[...] = low_iter[...]


def orthogonal(momentum):
    size = momentum.shape[0]
    return pl.pallas_call(
        newton_kernel,
        out_shape=jax.ShapeDtypeStruct((size, size), jnp.bfloat16),
        in_specs=[pl.BlockSpec(memory_space=pltpu.VMEM)],
        out_specs=pl.BlockSpec(memory_space=pltpu.VMEM),
        scratch_shapes=[
            pltpu.VMEM((size, size), jnp.float32),
            pltpu.VMEM((size, size), jnp.bfloat16),
            pltpu.VMEM((size, size), jnp.float32),
            pltpu.VMEM((size, size), jnp.bfloat16),
            pltpu.VMEM((size, size), jnp.bfloat16),
        ],
        compiler_params=pltpu.CompilerParams(vmem_limit_bytes=48 * 1024 * 1024),
        cost_estimate=pl.CostEstimate(
            flops=NEWTON_STEPS * 6 * size**3, bytes_accessed=6 * size * size, transcendentals=0
        ),
        name="newton",
    )(momentum)


def weight_grads(left, right, hidden_blocks, piece_rows):
    tokens, features = left.shape[1:]
    blocks = 4 + 2 * hidden_blocks
    half = features // 2
    group = half // piece_rows

    def left_at(block, part):
        early = jnp.where(block < 3, 0, jnp.where(block == 3, 1, 2))
        return jnp.where(block < 4 + hidden_blocks, early, block - 1 - hidden_blocks)

    def right_at(block, part):
        return jnp.minimum(block, 4 + hidden_blocks)

    def kernel(left_ref, right_ref, out_ref):
        product = contract_first(left_ref[0], right_ref[0])
        out_ref[...] = product.astype(jnp.bfloat16).reshape(group, 1, piece_rows, features)

    return pl.pallas_call(
        kernel,
        grid=(blocks, 2),
        out_shape=jax.ShapeDtypeStruct((2 * group, blocks, piece_rows, features), jnp.bfloat16),
        in_specs=[
            pl.BlockSpec((1, tokens, half), lambda b, p: (left_at(b, p), 0, p)),
            pl.BlockSpec((1, tokens, features), lambda b, p: (right_at(b, p), 0, 0)),
        ],
        out_specs=pl.BlockSpec((group, 1, piece_rows, features), lambda b, p: (p, b, 0, 0)),
        compiler_params=pltpu.CompilerParams(vmem_limit_bytes=48 * 1024 * 1024),
        cost_estimate=pl.CostEstimate(
            flops=2 * blocks * tokens * features**2,
            bytes_accessed=2 * blocks * features * (tokens + features),
            transcendentals=0,
        ),
        name="weight_grads",
    )(left, right)


def on_device(
    tokens,
    cotangent,
    slot_table,
    matrix_master,
    matrix_momentum,
    vector_params,
    vector_first,
    vector_second,
):
    features = tokens.shape[1]
    hidden_blocks = vector_params.shape[0] - 8
    slots = matrix_master.shape[0]
    owners = lax.axis_size("own")
    data_count = lax.axis_size("dp")
    slot_count = slots * owners
    f32 = jnp.float32
    gathered = lax.all_gather(matrix_master.astype(jnp.bfloat16), "own", axis=0, tiled=True)
    blocks = [
        lax.dynamic_index_in_dim(gathered, slot_table[place], 0, keepdims=False)
        for place in range(4 + 2 * hidden_blocks)
    ]
    w_query, w_key, w_value, w_out = blocks[:4]
    w_up = blocks[4 : 4 + hidden_blocks]
    w_down = blocks[4 + hidden_blocks :]

    def dot(left, right):
        return jnp.dot(left, right, preferred_element_type=f32)

    queries = (dot(tokens, w_query) + vector_params[0]).astype(jnp.bfloat16)
    key_rows = dot(tokens, w_key).astype(jnp.bfloat16)
    values = (dot(tokens, w_value) + vector_params[1]).astype(jnp.bfloat16)
    sequences = tokens.shape[0] // LEN
    triples = tuple(
        part.reshape(sequences, LEN, features) for part in (queries, key_rows, values)
    )
    mixed_rows, row_peak, row_total = lax.map(attend_forward, triples)
    mixed_rows = mixed_rows.reshape(sequences * LEN, features)
    attn_out = dot(mixed_rows, w_out) + vector_params[2]
    normed, norm_one_back = jax.vjp(
        layer_norm, tokens.astype(f32) + attn_out, vector_params[4], vector_params[5]
    )
    normed_low = normed.astype(jnp.bfloat16)
    activity, gelu_backs = [], []
    for place in range(hidden_blocks):
        full, back = jax.vjp(gelu_exact, dot(normed_low, w_up[place]) + vector_params[8 + place])
        activity.append(full.astype(jnp.bfloat16))
        gelu_backs.append(back)
    branch = vector_params[3]
    for place in range(hidden_blocks):
        branch = branch + dot(activity[place], w_down[place])
    output, norm_two_back = jax.vjp(layer_norm, normed + branch, vector_params[6], vector_params[7])
    d_resid_two, d_gain_two, d_shift_two = norm_two_back(cotangent.astype(f32))
    d_branch = d_resid_two.astype(jnp.bfloat16)
    d_hidden = [
        gelu_backs[place](contract_last(d_branch, w_down[place]))[0].astype(jnp.bfloat16)
        for place in range(hidden_blocks)
    ]
    d_normed = d_resid_two
    for place in range(hidden_blocks):
        d_normed = d_normed + contract_last(d_hidden[place], w_up[place])
    d_resid_one, d_gain_one, d_shift_one = norm_one_back(d_normed)
    d_attn = d_resid_one.astype(jnp.bfloat16)
    d_mixed = contract_last(d_attn, w_out).astype(jnp.bfloat16)
    bundle = triples + (d_mixed.reshape(sequences, LEN, features), row_peak, row_total)
    d_query, d_key, d_value = (
        part.reshape(sequences * LEN, features) for part in lax.map(attend_backward, bundle)
    )
    input_grad = (
        d_resid_one
        + contract_last(d_query, w_query)
        + contract_last(d_key, w_key)
        + contract_last(d_value, w_value)
    )
    left = jnp.stack([tokens, mixed_rows, normed_low] + activity)
    right = jnp.stack([d_query, d_key, d_value, d_attn] + d_hidden + [d_branch])
    devices = data_count * owners
    piece_rows = features // devices
    kernel_rows = max(piece_rows, 32)
    pieces = weight_grads(left, right, hidden_blocks, kernel_rows)
    if kernel_rows != piece_rows:
        finer = kernel_rows // piece_rows
        pieces = pieces.reshape(-1, pieces.shape[1], finer, piece_rows, features)
        pieces = pieces.transpose(0, 2, 1, 3, 4).reshape(devices, -1, piece_rows, features)
    share = lax.psum_scatter(pieces, ("dp", "own"), scatter_dimension=0, tiled=True)[0]

    def column_sum(part):
        return jnp.sum(part, axis=0, dtype=f32)

    vector_local = jnp.stack(
        [
            column_sum(d_query),
            column_sum(d_value),
            column_sum(d_attn),
            column_sum(d_branch),
            d_gain_one,
            d_shift_one,
            d_gain_two,
            d_shift_two,
        ]
        + [column_sum(part) for part in d_hidden]
    )
    vector_grad = jnp.sum(lax.all_gather(vector_local, ("dp", "own"), axis=0), axis=0)

    match = slot_table[None, :] == jnp.arange(slot_count, dtype=jnp.int32)[:, None]
    slot_used = jnp.any(match, axis=1)
    block_index = jnp.sum(
        jnp.where(match, jnp.arange(slot_table.shape[0], dtype=jnp.int32)[None, :], 0), axis=1
    )
    slot_share = jnp.stack(
        [lax.dynamic_index_in_dim(share, block_index[s], 0, keepdims=False) for s in range(slot_count)]
    ).reshape(owners, slots, piece_rows, features)
    mine = lax.all_to_all(slot_share, "own", split_axis=0, concat_axis=0, tiled=True)
    summed = lax.all_gather(mine, "dp", axis=0, tiled=False)
    summed = summed.transpose(2, 0, 1, 3, 4).reshape(slots, features, features).astype(f32)
    used_here = lax.dynamic_slice_in_dim(slot_used, lax.axis_index("own") * slots, slots)
    used_here = used_here[:, None, None]
    new_momentum = momentum_decay * matrix_momentum + jnp.where(used_here, summed, 0.0)

    copies = 1
    while copies * 2 * slots <= data_count:
        copies *= 2
    turn = lax.axis_index("dp")
    slot_place = jnp.minimum(turn // copies, slots - 1)
    ortho_low = orthogonal(
        lax.dynamic_index_in_dim(new_momentum, slot_place, 0, keepdims=False)
    )
    part_rows = features // copies
    ortho_part = lax.dynamic_slice_in_dim(ortho_low, (turn % copies) * part_rows, part_rows, 0)
    ortho = lax.all_gather(ortho_part, "dp", axis=0, tiled=True)[: slots * features]
    ortho = jnp.where(used_here, ortho.reshape(slots, features, features).astype(f32), 0.0)
    new_master = matrix_master - matrix_rate * (ortho + matrix_decay * matrix_master)
    new_first = beta_first * vector_first + (1.0 - beta_first) * vector_grad
    new_second = beta_second * vector_second + (1.0 - beta_second) * vector_grad * vector_grad
    first_hat = new_first / (1.0 - beta_first**STEP)
    second_hat = new_second / (1.0 - beta_second**STEP)
    new_params = vector_params - vector_rate * (
        first_hat / (jnp.sqrt(second_hat) + adam_epsilon) + vector_decay * vector_params
    )
    return (output, input_grad, new_master, new_momentum, new_params, new_first, new_second)


def solution(mesh):
    in_specs = (
        P(("dp", "own"), None),
        P(("dp", "own"), None),
        P(),
        P("own", None, None),
        P("own", None, None),
        P(),
        P(),
        P(),
    )
    out_specs = (
        P(("dp", "own"), None),
        P(("dp", "own"), None),
        P("own", None, None),
        P("own", None, None),
        P(),
        P(),
        P(),
    )
    return jax.shard_map(
        on_device, mesh=mesh, in_specs=in_specs, out_specs=out_specs, check_vma=False
    )
```

```python
import math

import jax
import jax.numpy as jnp
from jax import lax
from jax.experimental import pallas as pl
from jax.experimental.pallas import tpu as pltpu
from jax.sharding import PartitionSpec as P

HEADS = 16
HEAD = 64
LEN = 512
NEWTON_STEPS = 5
STEP = 10


poly_first = 3.4445
poly_second = -4.775
poly_third = 2.0315
momentum_decay = 0.95
matrix_rate = 1.0
matrix_decay = 0.01
beta_first = 0.9
beta_second = 0.999
vector_rate = 0.2
vector_decay = 0.01
adam_epsilon = 1e-08
norm_epsilon = 1e-05
ortho_epsilon = 1e-07


def layer_norm(values, gain_row, shift_row):
    centred = values - jnp.mean(values, axis=-1, keepdims=True)
    spread = jnp.mean(centred * centred, axis=-1, keepdims=True)
    return centred * lax.rsqrt(spread + norm_epsilon) * gain_row + shift_row


def gelu_exact(values):
    return 0.5 * values * (1.0 + jax.scipy.special.erf(values * (1.0 / math.sqrt(2.0))))


def contract_last(operand_left, operand_right):
    return lax.dot_general(
        operand_left, operand_right, (((1,), (1,)), ((), ())), preferred_element_type=jnp.float32
    )


def contract_first(operand_left, operand_right):
    return lax.dot_general(
        operand_left, operand_right, (((0,), (0,)), ((), ())), preferred_element_type=jnp.float32
    )


def head_scores(queries, key_rows):
    length = queries.shape[0]
    query_heads = queries.reshape(length, HEADS, HEAD)
    key_heads = key_rows.reshape(length, HEADS, HEAD)
    scores = jnp.einsum("qhd,khd->hqk", query_heads, key_heads, preferred_element_type=jnp.float32)
    return (scores * (1.0 / math.sqrt(HEAD)), query_heads, key_heads)


def attend_forward(triple):
    queries, key_rows, values = triple
    length = queries.shape[0]
    scores, query_heads, key_heads = head_scores(queries, key_rows)
    row_peak = jnp.max(scores, axis=-1, keepdims=True)
    exps = jnp.exp(scores - row_peak)
    row_total = jnp.sum(exps, axis=-1, keepdims=True)
    probabilities = (exps / row_total).astype(jnp.bfloat16)
    value_heads = values.reshape(length, HEADS, HEAD)
    mixed = jnp.einsum(
        "hqk,khd->qhd", probabilities, value_heads, preferred_element_type=jnp.float32
    )
    return (mixed.reshape(length, HEADS * HEAD).astype(jnp.bfloat16), row_peak, row_total)


def attend_backward(bundle):
    queries, key_rows, values, grad_mixed, row_peak, row_total = bundle
    length = queries.shape[0]
    scores, query_heads, key_heads = head_scores(queries, key_rows)
    probabilities = jnp.exp(scores - row_peak) / row_total
    value_heads = values.reshape(length, HEADS, HEAD)
    grad_heads = grad_mixed.reshape(length, HEADS, HEAD)
    grad_probs = jnp.einsum(
        "qhd,khd->hqk", grad_heads, value_heads, preferred_element_type=jnp.float32
    )
    row_dot = jnp.sum(grad_probs * probabilities, axis=-1, keepdims=True)
    grad_scores = (probabilities * (grad_probs - row_dot)).astype(jnp.bfloat16)
    scale = 1.0 / math.sqrt(HEAD)
    grad_query = (
        jnp.einsum("hqk,khd->qhd", grad_scores, key_heads, preferred_element_type=jnp.float32)
        * scale
    )
    grad_key = (
        jnp.einsum("hqk,qhd->khd", grad_scores, query_heads, preferred_element_type=jnp.float32)
        * scale
    )
    grad_value = jnp.einsum(
        "hqk,qhd->khd",
        probabilities.astype(jnp.bfloat16),
        grad_heads,
        preferred_element_type=jnp.float32,
    )
    features = HEADS * HEAD
    return tuple(
        grad.reshape(length, features).astype(jnp.bfloat16)
        for grad in (grad_query, grad_key, grad_value)
    )


def newton_kernel(momentum_ref, ortho_ref, iterate, low_iter, gram, gram_low, poly):
    size = momentum_ref.shape[0]
    tile = min(512, size)
    tiles = size // tile

    def total_step(place, total):
        rows = momentum_ref[pl.ds(pl.multiple_of(place * 128, 128), 128), :]
        return total + jnp.sum(rows * rows)

    total = lax.fori_loop(0, size // 128, total_step, jnp.float32(0.0))
    norm = jnp.sqrt(jnp.full((8, 128), total, jnp.float32)) + ortho_epsilon
    inverse = (1.0 / norm)[0:1, 0:1]

    def rows_at(place):
        return pl.ds(pl.multiple_of(place * tile, tile), tile)

    @pl.loop(0, tiles)
    def _(place):
        rows = rows_at(place)
        start = momentum_ref[rows, :] * inverse
        iterate[rows, :] = start
        low_iter[rows, :] = start.astype(jnp.bfloat16)

    @pl.loop(0, NEWTON_STEPS)
    def _(sweep):
        @pl.loop(0, tiles)
        def _(place):
            rows = rows_at(place)
            product = contract_last(low_iter[rows, :], low_iter[...])
            gram[rows, :] = product
            gram_low[rows, :] = product.astype(jnp.bfloat16)

        @pl.loop(0, tiles)
        def _(place):
            rows = rows_at(place)
            square = jnp.dot(
                gram_low[rows, :], gram_low[...], preferred_element_type=jnp.float32
            )
            poly[rows, :] = (poly_second * gram[rows, :] + poly_third * square).astype(
                jnp.bfloat16
            )

        @pl.loop(0, tiles)
        def _(place):
            rows = rows_at(place)
            iterate[rows, :] = poly_first * iterate[rows, :] + jnp.dot(
                poly[rows, :], low_iter[...], preferred_element_type=jnp.float32
            )

        @pl.loop(0, tiles)
        def _(place):
            rows = rows_at(place)
            low_iter[rows, :] = iterate[rows, :].astype(jnp.bfloat16)

    ortho_ref[...] = low_iter[...]


def orthogonal(momentum):
    size = momentum.shape[0]
    return pl.pallas_call(
        newton_kernel,
        out_shape=jax.ShapeDtypeStruct((size, size), jnp.bfloat16),
        in_specs=[pl.BlockSpec(memory_space=pltpu.VMEM)],
        out_specs=pl.BlockSpec(memory_space=pltpu.VMEM),
        scratch_shapes=[
            pltpu.VMEM((size, size), jnp.float32),
            pltpu.VMEM((size, size), jnp.bfloat16),
            pltpu.VMEM((size, size), jnp.float32),
            pltpu.VMEM((size, size), jnp.bfloat16),
            pltpu.VMEM((size, size), jnp.bfloat16),
        ],
        compiler_params=pltpu.CompilerParams(vmem_limit_bytes=48 * 1024 * 1024),
        cost_estimate=pl.CostEstimate(
            flops=NEWTON_STEPS * 6 * size**3, bytes_accessed=6 * size * size, transcendentals=0
        ),
        name="newton",
    )(momentum)


def weight_grads(left, right, left_at, right_at, blocks, piece_rows):
    tokens, features = left.shape[1:]
    half = features // 2
    group = half // piece_rows

    def kernel(left_ref, right_ref, out_ref):
        product = contract_first(left_ref[0], right_ref[0])
        out_ref[...] = product.astype(jnp.bfloat16).reshape(group, 1, piece_rows, features)

    return pl.pallas_call(
        kernel,
        grid=(blocks, 2),
        out_shape=jax.ShapeDtypeStruct((2 * group, blocks, piece_rows, features), jnp.bfloat16),
        in_specs=[
            pl.BlockSpec((1, tokens, half), lambda b, p: (left_at(b), 0, p)),
            pl.BlockSpec((1, tokens, features), lambda b, p: (right_at(b), 0, 0)),
        ],
        out_specs=pl.BlockSpec((group, 1, piece_rows, features), lambda b, p: (p, b, 0, 0)),
        compiler_params=pltpu.CompilerParams(vmem_limit_bytes=48 * 1024 * 1024),
        cost_estimate=pl.CostEstimate(
            flops=2 * blocks * tokens * features**2,
            bytes_accessed=2 * blocks * features * (tokens + features),
            transcendentals=0,
        ),
        name="weight_grads",
    )(left, right)


def chip_sum(pieces, piece_rows):
    owners = lax.axis_size("own")
    kernel_rows = pieces.shape[2]
    if kernel_rows != piece_rows:
        finer = kernel_rows // piece_rows
        pieces = pieces.reshape(pieces.shape[0], -1, finer, piece_rows, pieces.shape[3])
        pieces = pieces.transpose(0, 2, 1, 3, 4).reshape(
            pieces.shape[0] * finer, -1, piece_rows, pieces.shape[4]
        )
    if owners != 2:
        return lax.psum_scatter(pieces, "own", scatter_dimension=0, tiled=True)
    halves = pieces.reshape((owners, -1) + pieces.shape[1:])
    me = lax.axis_index("own")
    kept = lax.dynamic_index_in_dim(halves, me, 0, keepdims=False)
    sent = lax.dynamic_index_in_dim(halves, 1 - me, 0, keepdims=False)
    got = lax.ppermute(sent, "own", [(0, 1), (1, 0)])
    return (kept.astype(jnp.float32) + got.astype(jnp.float32)).astype(jnp.bfloat16)


def on_device(
    tokens,
    cotangent,
    slot_table,
    matrix_master,
    matrix_momentum,
    vector_params,
    vector_first,
    vector_second,
):
    features = tokens.shape[1]
    hidden_blocks = vector_params.shape[0] - 8
    slots = matrix_master.shape[0]
    owners = lax.axis_size("own")
    data_count = lax.axis_size("dp")
    slot_count = slots * owners
    f32 = jnp.float32
    gathered = lax.all_gather(matrix_master.astype(jnp.bfloat16), "own", axis=0, tiled=True)
    blocks = [
        lax.dynamic_index_in_dim(gathered, slot_table[place], 0, keepdims=False)
        for place in range(4 + 2 * hidden_blocks)
    ]
    w_query, w_key, w_value, w_out = blocks[:4]
    w_up = blocks[4 : 4 + hidden_blocks]
    w_down = blocks[4 + hidden_blocks :]

    def dot(left, right):
        return jnp.dot(left, right, preferred_element_type=f32)

    queries = (dot(tokens, w_query) + vector_params[0]).astype(jnp.bfloat16)
    key_rows = dot(tokens, w_key).astype(jnp.bfloat16)
    values = (dot(tokens, w_value) + vector_params[1]).astype(jnp.bfloat16)
    sequences = tokens.shape[0] // LEN
    triples = tuple(
        part.reshape(sequences, LEN, features) for part in (queries, key_rows, values)
    )
    mixed_rows, row_peak, row_total = lax.map(attend_forward, triples)
    mixed_rows = mixed_rows.reshape(sequences * LEN, features)
    attn_out = dot(mixed_rows, w_out) + vector_params[2]
    normed, norm_one_back = jax.vjp(
        layer_norm, tokens.astype(f32) + attn_out, vector_params[4], vector_params[5]
    )
    normed_low = normed.astype(jnp.bfloat16)
    activity, gelu_backs = [], []
    for place in range(hidden_blocks):
        full, back = jax.vjp(gelu_exact, dot(normed_low, w_up[place]) + vector_params[8 + place])
        activity.append(full.astype(jnp.bfloat16))
        gelu_backs.append(back)
    branch = vector_params[3]
    for place in range(hidden_blocks):
        branch = branch + dot(activity[place], w_down[place])
    output, norm_two_back = jax.vjp(layer_norm, normed + branch, vector_params[6], vector_params[7])
    d_resid_two, d_gain_two, d_shift_two = norm_two_back(cotangent.astype(f32))
    d_branch = d_resid_two.astype(jnp.bfloat16)
    d_hidden = [
        gelu_backs[place](contract_last(d_branch, w_down[place]))[0].astype(jnp.bfloat16)
        for place in range(hidden_blocks)
    ]
    d_normed = d_resid_two
    for place in range(hidden_blocks):
        d_normed = d_normed + contract_last(d_hidden[place], w_up[place])
    d_resid_one, d_gain_one, d_shift_one = norm_one_back(d_normed)
    d_attn = d_resid_one.astype(jnp.bfloat16)
    devices = data_count * owners
    piece_rows = features // devices
    kernel_rows = max(piece_rows, 32)
    feed_pieces = weight_grads(
        jnp.stack([normed_low] + activity),
        jnp.stack(d_hidden + [d_branch]),
        lambda place: jnp.maximum(place + 1 - hidden_blocks, 0),
        lambda place: jnp.minimum(place, hidden_blocks),
        2 * hidden_blocks,
        kernel_rows,
    )
    d_attn, feed_pieces = lax.optimization_barrier((d_attn, feed_pieces))
    feed_sum = chip_sum(feed_pieces, piece_rows)
    feed_share = lax.psum_scatter(feed_sum, "dp", scatter_dimension=0, tiled=True)[0]
    d_mixed = contract_last(d_attn, w_out).astype(jnp.bfloat16)
    bundle = triples + (d_mixed.reshape(sequences, LEN, features), row_peak, row_total)
    d_query, d_key, d_value = (
        part.reshape(sequences * LEN, features) for part in lax.map(attend_backward, bundle)
    )
    d_query, d_key, d_value, feed_sum = lax.optimization_barrier(
        (d_query, d_key, d_value, feed_sum)
    )
    attn_pieces = weight_grads(
        jnp.stack([tokens, mixed_rows]),
        jnp.stack([d_query, d_key, d_value, d_attn]),
        lambda place: place // 3,
        lambda place: place,
        4,
        kernel_rows,
    )
    attn_sum = chip_sum(attn_pieces, piece_rows)
    attn_share = lax.psum_scatter(attn_sum, "dp", scatter_dimension=0, tiled=True)[0]
    share = jnp.concatenate([attn_share, feed_share], axis=0)
    input_grad = (
        d_resid_one
        + contract_last(d_query, w_query)
        + contract_last(d_key, w_key)
        + contract_last(d_value, w_value)
    )
    def column_sum(part):
        return jnp.sum(part, axis=0, dtype=f32)

    vector_local = jnp.stack(
        [
            column_sum(d_query),
            column_sum(d_value),
            column_sum(d_attn),
            column_sum(d_branch),
            d_gain_one,
            d_shift_one,
            d_gain_two,
            d_shift_two,
        ]
        + [column_sum(part) for part in d_hidden]
    )
    vector_chip = lax.psum(vector_local, "own").astype(jnp.bfloat16)

    match = slot_table[None, :] == jnp.arange(slot_count, dtype=jnp.int32)[:, None]
    slot_used = jnp.any(match, axis=1)
    block_index = jnp.sum(
        jnp.where(match, jnp.arange(slot_table.shape[0], dtype=jnp.int32)[None, :], 0), axis=1
    )
    slot_share = jnp.stack(
        [lax.dynamic_index_in_dim(share, block_index[s], 0, keepdims=False) for s in range(slot_count)]
    ).reshape(owners, slots, piece_rows, features)
    mine = lax.all_to_all(slot_share, "own", split_axis=0, concat_axis=0, tiled=True)
    rows_here = owners * slots * piece_rows
    vector_rows = vector_chip.shape[0]
    padded = -(-(rows_here + vector_rows) // 16) * 16
    outgoing = jnp.concatenate(
        [
            mine.reshape(rows_here, features),
            vector_chip,
            jnp.zeros((padded - rows_here - vector_rows, features), jnp.bfloat16),
        ],
        axis=0,
    )
    incoming = lax.all_gather(outgoing, "dp", axis=0, tiled=False)
    vector_grad = jnp.sum(
        incoming[:, rows_here : rows_here + vector_rows].astype(f32), axis=0
    )
    summed = incoming[:, :rows_here].reshape(data_count, owners, slots, piece_rows, features)
    summed = summed.transpose(2, 1, 0, 3, 4).reshape(slots, features, features).astype(f32)
    used_here = lax.dynamic_slice_in_dim(slot_used, lax.axis_index("own") * slots, slots)
    used_here = used_here[:, None, None]
    new_momentum = momentum_decay * matrix_momentum + jnp.where(used_here, summed, 0.0)

    copies = 1
    while copies * 2 * slots <= data_count:
        copies *= 2
    turn = lax.axis_index("dp")
    place_of = [min(index // copies, slots - 1) for index in range(data_count)]
    by_turn = jnp.stack([mine[:, place] for place in place_of])
    my_rows = lax.all_to_all(by_turn, "dp", split_axis=0, concat_axis=0, tiled=True)
    my_summed = my_rows.transpose(1, 0, 2, 3).reshape(features, features).astype(f32)
    slot_place = jnp.minimum(turn // copies, slots - 1)
    my_momentum = lax.dynamic_index_in_dim(matrix_momentum, slot_place, 0, keepdims=False)
    ortho_low = orthogonal(momentum_decay * my_momentum + my_summed)
    part_rows = features // copies
    ortho_part = lax.dynamic_slice_in_dim(ortho_low, (turn % copies) * part_rows, part_rows, 0)
    ortho = lax.all_gather(ortho_part, "dp", axis=0, tiled=True)[: slots * features]
    ortho = jnp.where(used_here, ortho.reshape(slots, features, features).astype(f32), 0.0)
    new_master = matrix_master - matrix_rate * (ortho + matrix_decay * matrix_master)
    new_first = beta_first * vector_first + (1.0 - beta_first) * vector_grad
    new_second = beta_second * vector_second + (1.0 - beta_second) * vector_grad * vector_grad
    first_hat = new_first / (1.0 - beta_first**STEP)
    second_hat = new_second / (1.0 - beta_second**STEP)
    new_params = vector_params - vector_rate * (
        first_hat / (jnp.sqrt(second_hat) + adam_epsilon) + vector_decay * vector_params
    )
    return (output, input_grad, new_master, new_momentum, new_params, new_first, new_second)


def solution(mesh):
    in_specs = (
        P(("dp", "own"), None),
        P(("dp", "own"), None),
        P(),
        P("own", None, None),
        P("own", None, None),
        P(),
        P(),
        P(),
    )
    out_specs = (
        P(("dp", "own"), None),
        P(("dp", "own"), None),
        P("own", None, None),
        P("own", None, None),
        P(),
        P(),
        P(),
    )
    return jax.shard_map(
        on_device, mesh=mesh, in_specs=in_specs, out_specs=out_specs, check_vma=False
    )
```

```python
import math

import jax
import jax.numpy as jnp
from jax import lax
from jax.experimental import pallas as pl
from jax.experimental.pallas import tpu as pltpu
from jax.sharding import PartitionSpec as P

HEADS = 16
HEAD = 64
LEN = 512
NEWTON_STEPS = 5
STEP = 10


poly_first = 3.4445
poly_second = -4.775
poly_third = 2.0315
momentum_decay = 0.95
matrix_rate = 1.0
matrix_decay = 0.01
beta_first = 0.9
beta_second = 0.999
vector_rate = 0.2
vector_decay = 0.01
adam_epsilon = 1e-08
norm_epsilon = 1e-05
ortho_epsilon = 1e-07


def layer_norm(values, gain_row, shift_row):
    centred = values - jnp.mean(values, axis=-1, keepdims=True)
    spread = jnp.mean(centred * centred, axis=-1, keepdims=True)
    return centred * lax.rsqrt(spread + norm_epsilon) * gain_row + shift_row


def gelu_exact(values):
    return 0.5 * values * (1.0 + jax.scipy.special.erf(values * (1.0 / math.sqrt(2.0))))


def contract_last(operand_left, operand_right):
    return lax.dot_general(
        operand_left, operand_right, (((1,), (1,)), ((), ())), preferred_element_type=jnp.float32
    )


def contract_first(operand_left, operand_right):
    return lax.dot_general(
        operand_left, operand_right, (((0,), (0,)), ((), ())), preferred_element_type=jnp.float32
    )


def head_scores(queries, key_rows):
    length = queries.shape[0]
    query_heads = queries.reshape(length, HEADS, HEAD)
    key_heads = key_rows.reshape(length, HEADS, HEAD)
    scores = jnp.einsum("qhd,khd->hqk", query_heads, key_heads, preferred_element_type=jnp.float32)
    return (scores * (1.0 / math.sqrt(HEAD)), query_heads, key_heads)


def attend_forward(triple):
    queries, key_rows, values = triple
    length = queries.shape[0]
    scores, query_heads, key_heads = head_scores(queries, key_rows)
    row_peak = jnp.max(scores, axis=-1, keepdims=True)
    exps = jnp.exp(scores - row_peak)
    row_total = jnp.sum(exps, axis=-1, keepdims=True)
    probabilities = (exps / row_total).astype(jnp.bfloat16)
    value_heads = values.reshape(length, HEADS, HEAD)
    mixed = jnp.einsum(
        "hqk,khd->qhd", probabilities, value_heads, preferred_element_type=jnp.float32
    )
    return (mixed.reshape(length, HEADS * HEAD).astype(jnp.bfloat16), row_peak, row_total)


def attend_backward(bundle):
    queries, key_rows, values, grad_mixed, row_peak, row_total = bundle
    length = queries.shape[0]
    scores, query_heads, key_heads = head_scores(queries, key_rows)
    probabilities = jnp.exp(scores - row_peak) / row_total
    value_heads = values.reshape(length, HEADS, HEAD)
    grad_heads = grad_mixed.reshape(length, HEADS, HEAD)
    grad_probs = jnp.einsum(
        "qhd,khd->hqk", grad_heads, value_heads, preferred_element_type=jnp.float32
    )
    row_dot = jnp.sum(grad_probs * probabilities, axis=-1, keepdims=True)
    grad_scores = (probabilities * (grad_probs - row_dot)).astype(jnp.bfloat16)
    scale = 1.0 / math.sqrt(HEAD)
    grad_query = (
        jnp.einsum("hqk,khd->qhd", grad_scores, key_heads, preferred_element_type=jnp.float32)
        * scale
    )
    grad_key = (
        jnp.einsum("hqk,qhd->khd", grad_scores, query_heads, preferred_element_type=jnp.float32)
        * scale
    )
    grad_value = jnp.einsum(
        "hqk,qhd->khd",
        probabilities.astype(jnp.bfloat16),
        grad_heads,
        preferred_element_type=jnp.float32,
    )
    features = HEADS * HEAD
    return tuple(
        grad.reshape(length, features).astype(jnp.bfloat16)
        for grad in (grad_query, grad_key, grad_value)
    )


def newton_kernel(momentum_ref, ortho_ref, iterate, low_iter, gram, gram_low, poly):
    size = momentum_ref.shape[0]
    tile = min(512, size)
    tiles = size // tile

    def total_step(place, total):
        rows = momentum_ref[pl.ds(pl.multiple_of(place * 128, 128), 128), :]
        return total + jnp.sum(rows * rows)

    total = lax.fori_loop(0, size // 128, total_step, jnp.float32(0.0))
    norm = jnp.sqrt(jnp.full((8, 128), total, jnp.float32)) + ortho_epsilon
    inverse = (1.0 / norm)[0:1, 0:1]

    def rows_at(place):
        return pl.ds(pl.multiple_of(place * tile, tile), tile)

    @pl.loop(0, tiles)
    def _(place):
        rows = rows_at(place)
        start = momentum_ref[rows, :] * inverse
        iterate[rows, :] = start
        low_iter[rows, :] = start.astype(jnp.bfloat16)

    @pl.loop(0, NEWTON_STEPS)
    def _(sweep):
        @pl.loop(0, tiles)
        def _(place):
            rows = rows_at(place)
            product = contract_last(low_iter[rows, :], low_iter[...])
            gram[rows, :] = product
            gram_low[rows, :] = product.astype(jnp.bfloat16)

        @pl.loop(0, tiles)
        def _(place):
            rows = rows_at(place)
            square = jnp.dot(
                gram_low[rows, :], gram_low[...], preferred_element_type=jnp.float32
            )
            poly[rows, :] = (poly_second * gram[rows, :] + poly_third * square).astype(
                jnp.bfloat16
            )

        @pl.loop(0, tiles)
        def _(place):
            rows = rows_at(place)
            iterate[rows, :] = poly_first * iterate[rows, :] + jnp.dot(
                poly[rows, :], low_iter[...], preferred_element_type=jnp.float32
            )

        @pl.loop(0, tiles)
        def _(place):
            rows = rows_at(place)
            low_iter[rows, :] = iterate[rows, :].astype(jnp.bfloat16)

    ortho_ref[...] = low_iter[...]


def orthogonal(momentum):
    size = momentum.shape[0]
    return pl.pallas_call(
        newton_kernel,
        out_shape=jax.ShapeDtypeStruct((size, size), jnp.bfloat16),
        in_specs=[pl.BlockSpec(memory_space=pltpu.VMEM)],
        out_specs=pl.BlockSpec(memory_space=pltpu.VMEM),
        scratch_shapes=[
            pltpu.VMEM((size, size), jnp.float32),
            pltpu.VMEM((size, size), jnp.bfloat16),
            pltpu.VMEM((size, size), jnp.float32),
            pltpu.VMEM((size, size), jnp.bfloat16),
            pltpu.VMEM((size, size), jnp.bfloat16),
        ],
        compiler_params=pltpu.CompilerParams(vmem_limit_bytes=48 * 1024 * 1024),
        cost_estimate=pl.CostEstimate(
            flops=NEWTON_STEPS * 6 * size**3, bytes_accessed=6 * size * size, transcendentals=0
        ),
        name="newton",
    )(momentum)


def weight_grads(left, right, left_at, right_at, blocks, piece_rows):
    tokens, features = left.shape[1:]
    half = features // 2
    group = half // piece_rows

    def kernel(left_ref, right_ref, out_ref):
        product = contract_first(left_ref[0], right_ref[0])
        out_ref[...] = product.astype(jnp.bfloat16).reshape(group, 1, piece_rows, features)

    return pl.pallas_call(
        kernel,
        grid=(blocks, 2),
        out_shape=jax.ShapeDtypeStruct((2 * group, blocks, piece_rows, features), jnp.bfloat16),
        in_specs=[
            pl.BlockSpec((1, tokens, half), lambda b, p: (left_at(b), 0, p)),
            pl.BlockSpec((1, tokens, features), lambda b, p: (right_at(b), 0, 0)),
        ],
        out_specs=pl.BlockSpec((group, 1, piece_rows, features), lambda b, p: (p, b, 0, 0)),
        compiler_params=pltpu.CompilerParams(vmem_limit_bytes=48 * 1024 * 1024),
        cost_estimate=pl.CostEstimate(
            flops=2 * blocks * tokens * features**2,
            bytes_accessed=2 * blocks * features * (tokens + features),
            transcendentals=0,
        ),
        name="weight_grads",
    )(left, right)


def scatter_sum(pieces, piece_rows, devices):
    kernel_rows = pieces.shape[2]
    if kernel_rows != piece_rows:
        finer = kernel_rows // piece_rows
        pieces = pieces.reshape(pieces.shape[0], -1, finer, piece_rows, pieces.shape[3])
        pieces = pieces.transpose(0, 2, 1, 3, 4).reshape(devices, -1, piece_rows, pieces.shape[4])
    return lax.psum_scatter(pieces, ("dp", "own"), scatter_dimension=0, tiled=True)[0]


def on_device(
    tokens,
    cotangent,
    slot_table,
    matrix_master,
    matrix_momentum,
    vector_params,
    vector_first,
    vector_second,
):
    features = tokens.shape[1]
    hidden_blocks = vector_params.shape[0] - 8
    slots = matrix_master.shape[0]
    owners = lax.axis_size("own")
    data_count = lax.axis_size("dp")
    slot_count = slots * owners
    f32 = jnp.float32
    gathered = lax.all_gather(matrix_master.astype(jnp.bfloat16), "own", axis=0, tiled=True)
    blocks = [
        lax.dynamic_index_in_dim(gathered, slot_table[place], 0, keepdims=False)
        for place in range(4 + 2 * hidden_blocks)
    ]
    w_query, w_key, w_value, w_out = blocks[:4]
    w_up = blocks[4 : 4 + hidden_blocks]
    w_down = blocks[4 + hidden_blocks :]

    def dot(left, right):
        return jnp.dot(left, right, preferred_element_type=f32)

    queries = (dot(tokens, w_query) + vector_params[0]).astype(jnp.bfloat16)
    key_rows = dot(tokens, w_key).astype(jnp.bfloat16)
    values = (dot(tokens, w_value) + vector_params[1]).astype(jnp.bfloat16)
    sequences = tokens.shape[0] // LEN
    triples = tuple(
        part.reshape(sequences, LEN, features) for part in (queries, key_rows, values)
    )
    mixed_rows, row_peak, row_total = lax.map(attend_forward, triples)
    mixed_rows = mixed_rows.reshape(sequences * LEN, features)
    attn_out = dot(mixed_rows, w_out) + vector_params[2]
    normed, norm_one_back = jax.vjp(
        layer_norm, tokens.astype(f32) + attn_out, vector_params[4], vector_params[5]
    )
    normed_low = normed.astype(jnp.bfloat16)
    activity, gelu_backs = [], []
    for place in range(hidden_blocks):
        full, back = jax.vjp(gelu_exact, dot(normed_low, w_up[place]) + vector_params[8 + place])
        activity.append(full.astype(jnp.bfloat16))
        gelu_backs.append(back)
    branch = vector_params[3]
    for place in range(hidden_blocks):
        branch = branch + dot(activity[place], w_down[place])
    output, norm_two_back = jax.vjp(layer_norm, normed + branch, vector_params[6], vector_params[7])
    d_resid_two, d_gain_two, d_shift_two = norm_two_back(cotangent.astype(f32))
    d_branch = d_resid_two.astype(jnp.bfloat16)
    d_hidden = [
        gelu_backs[place](contract_last(d_branch, w_down[place]))[0].astype(jnp.bfloat16)
        for place in range(hidden_blocks)
    ]
    d_normed = d_resid_two
    for place in range(hidden_blocks):
        d_normed = d_normed + contract_last(d_hidden[place], w_up[place])
    d_resid_one, d_gain_one, d_shift_one = norm_one_back(d_normed)
    d_attn = d_resid_one.astype(jnp.bfloat16)
    devices = data_count * owners
    piece_rows = features // devices
    kernel_rows = max(piece_rows, 32)
    feed_pieces = weight_grads(
        jnp.stack([normed_low] + activity),
        jnp.stack(d_hidden + [d_branch]),
        lambda place: jnp.maximum(place + 1 - hidden_blocks, 0),
        lambda place: jnp.minimum(place, hidden_blocks),
        2 * hidden_blocks,
        kernel_rows,
    )
    d_attn, feed_pieces = lax.optimization_barrier((d_attn, feed_pieces))
    feed_share = scatter_sum(feed_pieces, piece_rows, devices)
    d_mixed = contract_last(d_attn, w_out).astype(jnp.bfloat16)
    bundle = triples + (d_mixed.reshape(sequences, LEN, features), row_peak, row_total)
    d_query, d_key, d_value = (
        part.reshape(sequences * LEN, features) for part in lax.map(attend_backward, bundle)
    )
    attn_pieces = weight_grads(
        jnp.stack([tokens, mixed_rows]),
        jnp.stack([d_query, d_key, d_value, d_attn]),
        lambda place: place // 3,
        lambda place: place,
        4,
        kernel_rows,
    )
    input_grad = (
        d_resid_one
        + contract_last(d_query, w_query)
        + contract_last(d_key, w_key)
        + contract_last(d_value, w_value)
    )
    def column_sum(part):
        return jnp.sum(part, axis=0, dtype=f32)

    vector_local = jnp.stack(
        [
            column_sum(d_query),
            column_sum(d_value),
            column_sum(d_attn),
            column_sum(d_branch),
            d_gain_one,
            d_shift_one,
            d_gain_two,
            d_shift_two,
        ]
        + [column_sum(part) for part in d_hidden]
    )
    vector_grad = lax.psum(vector_local, ("dp", "own"))
    attn_pieces, feed_share, vector_grad = lax.optimization_barrier(
        (attn_pieces, feed_share, vector_grad)
    )
    attn_share = scatter_sum(attn_pieces, piece_rows, devices)
    share = jnp.concatenate([attn_share, feed_share], axis=0)

    match = slot_table[None, :] == jnp.arange(slot_count, dtype=jnp.int32)[:, None]
    slot_used = jnp.any(match, axis=1)
    block_index = jnp.sum(
        jnp.where(match, jnp.arange(slot_table.shape[0], dtype=jnp.int32)[None, :], 0), axis=1
    )
    slot_share = jnp.stack(
        [lax.dynamic_index_in_dim(share, block_index[s], 0, keepdims=False) for s in range(slot_count)]
    ).reshape(owners, slots, piece_rows, features)
    mine = lax.all_to_all(slot_share, "own", split_axis=0, concat_axis=0, tiled=True)
    summed = lax.all_gather(mine, "dp", axis=0, tiled=False)
    summed = summed.transpose(2, 0, 1, 3, 4).reshape(slots, features, features).astype(f32)
    used_here = lax.dynamic_slice_in_dim(slot_used, lax.axis_index("own") * slots, slots)
    used_here = used_here[:, None, None]
    new_momentum = momentum_decay * matrix_momentum + jnp.where(used_here, summed, 0.0)

    copies = 1
    while copies * 2 * slots <= data_count:
        copies *= 2
    turn = lax.axis_index("dp")
    place_of = [min(index // copies, slots - 1) for index in range(data_count)]
    by_turn = jnp.stack([mine[:, place] for place in place_of])
    my_rows = lax.all_to_all(by_turn, "dp", split_axis=0, concat_axis=0, tiled=True)
    my_summed = my_rows.reshape(features, features).astype(f32)
    slot_place = jnp.minimum(turn // copies, slots - 1)
    my_momentum = lax.dynamic_index_in_dim(matrix_momentum, slot_place, 0, keepdims=False)
    ortho_low = orthogonal(momentum_decay * my_momentum + my_summed)
    part_rows = features // copies
    ortho_part = lax.dynamic_slice_in_dim(ortho_low, (turn % copies) * part_rows, part_rows, 0)
    ortho = lax.all_gather(ortho_part, "dp", axis=0, tiled=True)
    ortho, new_momentum = lax.optimization_barrier((ortho, new_momentum))
    ortho = ortho[: slots * features]
    ortho = jnp.where(used_here, ortho.reshape(slots, features, features).astype(f32), 0.0)
    new_master = matrix_master - matrix_rate * (ortho + matrix_decay * matrix_master)
    new_first = beta_first * vector_first + (1.0 - beta_first) * vector_grad
    new_second = beta_second * vector_second + (1.0 - beta_second) * vector_grad * vector_grad
    first_hat = new_first / (1.0 - beta_first**STEP)
    second_hat = new_second / (1.0 - beta_second**STEP)
    new_params = vector_params - vector_rate * (
        first_hat / (jnp.sqrt(second_hat) + adam_epsilon) + vector_decay * vector_params
    )
    return (output, input_grad, new_master, new_momentum, new_params, new_first, new_second)


def solution(mesh):
    in_specs = (
        P(("dp", "own"), None),
        P(("dp", "own"), None),
        P(),
        P("own", None, None),
        P("own", None, None),
        P(),
        P(),
        P(),
    )
    out_specs = (
        P(("dp", "own"), None),
        P(("dp", "own"), None),
        P("own", None, None),
        P("own", None, None),
        P(),
        P(),
        P(),
    )
    return jax.shard_map(
        on_device, mesh=mesh, in_specs=in_specs, out_specs=out_specs, check_vma=False
    )
```
